256 devices in a mesh: pts: 128 (over x, z, y), blk: 2 (over core).
Axes of the slice: x: 4, y: 4, z: 8, core: 2. Of those that a mesh axis runs over, the one named last changes fastest.
Arguments:
- basis_values: bfloat16 [512, 4096, 512], P(('pts', 'blk')), may hold values from -6 to 6
- density: bfloat16 [65536, 1536], P(('pts', 'blk')), may hold values from -0.01171875 to 0.01171875
- sig_blocks: int32 [512, 4], P(('pts', 'blk')), may hold values from 0 to 511, as said below
- grid_weights: float32 [512, 4096], P(('pts', 'blk')), may hold values from 0.002 to 0.02
- atom_of: int32 [512, 4096], P(('pts', 'blk')), may hold values from 0 to 4095, as said below
- in_weight: float32 [256], replicated, may hold values from -4 to 4
- in_bias: float32 [256], replicated, may hold values from -3 to 3
- atom_proj: bfloat16 [256, 64], replicated, may hold values from -0.375 to 0.375
- hidden_weight: bfloat16 [256, 256], replicated, may hold values from -0.375 to 0.375
- atom_in: bfloat16 [64, 256], replicated, may hold values from -0.75 to 0.75
- hidden_bias: float32 [256], replicated, may hold values from -3 to 3
- out_weight: bfloat16 [256], replicated, may hold values from -0.375 to 0.375
Outputs:
- potential: float32 [65536, 1536], P(('pts', 'blk'))
The draws below stay inside these ranges and needn't reach their ends.
Inputs may be any that keep to these rules, and one draw needn't show every extreme that they name: `sig_blocks`: batch b lies on chip c = b // 4; its 4 blocks are distinct and lie in blocks 4 * (c - 1) to 4 * (c + 2) - 1. `atom_of`: every point of batch b, on chip c = b // 4, belongs to one of atoms 32 * (c - 1) to 32 * (c + 2) - 1.
All inputs are finite; a program needn't handle non-finite values.
Results may differ from the reference program's by a relative error of at most 0.0034.
Values may be sent and summed in bfloat16 or wider, within the bound.
No kernel may reach another device: no remote copies, remote signals or barrier semaphores. Data moves between devices by JAX's collectives and lax.ppermute only.
A program may use at most 128 MiB of HBM per device.

```python
import math
import jax
import jax.numpy as jnp
from jax import lax

FB = 128
SIGB = 4
PTS_B = 4096
HID = 256
ATW = 64
SIGF = 512
CHIPB = 4
WINF = 1536
NB = 512
NFUNC = 65536
NBATCH = 512
BPC = 4
CHIPA = 32
NATOM = 4096


def draw_sig_blocks(key, part):
    chip_of = jnp.arange(NBATCH, dtype=jnp.int32) // BPC
    offsets = jnp.arange(3 * CHIPB, dtype=jnp.int32)
    candidates = CHIPB * (chip_of[:, None] - 1) + offsets[None, :]
    inside = (candidates >= 0) & (candidates < NB)
    scores = jax.random.randint(jax.random.fold_in(key, 11), (NBATCH, 3 * CHIPB), 0, 2 ** 20) * 64 + offsets[None, :]
    scores = scores + jnp.where(inside, 0, 2 ** 28)
    order = jnp.argsort(scores, axis=1)
    picked = jnp.take_along_axis(candidates, order[:, :SIGB], axis=1)
    return picked.astype(jnp.int32)


def draw_atom_of(key, part):
    chip_of = jnp.arange(NBATCH, dtype=jnp.int32) // BPC
    lowest = jnp.maximum(CHIPA * (chip_of - 1), 0)
    highest = jnp.minimum(CHIPA * (chip_of + 2), NATOM)
    lowest = jnp.broadcast_to(lowest[:, None], (NBATCH, PTS_B))
    highest = jnp.broadcast_to(highest[:, None], (NBATCH, PTS_B))
    return jax.random.randint(jax.random.fold_in(key, 23), (NBATCH, PTS_B), lowest, highest).astype(jnp.int32)


def block_levels(key, dims, pieces, smallest, top_value):
    def one(position, shards_of):
        heights = jax.random.uniform(jax.random.fold_in(jax.random.fold_in(key, 6), position), (shards_of,), jnp.float32, smallest / len(pieces), top_value / len(pieces))
        return jnp.repeat(jnp.exp(heights), dims[position] // shards_of).reshape((-1,) + (1,) * (len(dims) - position - 1))

    factor_of = one(*pieces[0])
    for cut in pieces[1:]:
        factor_of = factor_of * one(*cut)
    return factor_of


def centred(own_key, extent, deviation, limit, shards=(), kind=jnp.bfloat16):
    entries = deviation * jax.random.normal(own_key, extent, jnp.float32)
    if shards:
        entries = entries * block_levels(own_key, extent, shards, -0.22, 0.18)
    return jnp.clip(entries, -limit, limit).astype(kind)


def setup_inputs(seed: int = 0) -> dict:
    key_list = jax.random.split(jax.random.key(seed), 13)
    basis_values = centred(key_list[0], (NBATCH, PTS_B, SIGF), 1.0, 6.0, ((0, 256),))
    density = centred(key_list[1], (NFUNC, WINF), (SIGF * SIGF) ** -0.5, 0.01171875, ((0, 256),))
    sig_blocks = draw_sig_blocks(jax.random.fold_in(key_list[12], 71), 0)
    grid_weights = jnp.clip(jnp.exp(math.log(0.02) - 2.30258502 * jax.random.uniform(key_list[3], (NBATCH, PTS_B), jnp.float32) ** block_levels(key_list[3], (NBATCH, PTS_B), ((0, 256),), -0.2, 0.2)), 0.002, 0.02)
    atom_of = draw_atom_of(jax.random.fold_in(key_list[12], 71), 0)
    in_weight = centred(key_list[5], (HID,), 1.0, 4.0, (), jnp.float32)
    in_bias = centred(key_list[6], (HID,), 0.5, 3.0, (), jnp.float32)
    atom_proj = centred(key_list[7], (HID, ATW), HID ** -0.5, 0.375)
    hidden_weight = centred(key_list[8], (HID, HID), HID ** -0.5, 0.375)
    atom_in = centred(key_list[9], (ATW, HID), ATW ** -0.5, 0.75)
    hidden_bias = centred(key_list[10], (HID,), 0.5, 3.0, (), jnp.float32)
    out_weight = centred(key_list[11], (HID,), HID ** -0.5, 0.375)
    return dict(basis_values=basis_values, density=density, sig_blocks=sig_blocks, grid_weights=grid_weights, atom_of=atom_of, in_weight=in_weight, in_bias=in_bias, atom_proj=atom_proj, hidden_weight=hidden_weight, atom_in=atom_in, hidden_bias=hidden_bias, out_weight=out_weight)


eps_atom = 0.0001

def batch_density(density, blocks):
    chip_of = blocks // CHIPB
    row_parts = []
    for row_slot in range(SIGB):
        col_parts = []
        for col_slot in range(SIGB):
            start_col = blocks[col_slot] - CHIPB * (chip_of[row_slot] - 1)
            inside = jnp.abs(chip_of[col_slot] - chip_of[row_slot]) <= 1
            start_col = jnp.clip(start_col, 0, 3 * CHIPB - 1)
            block_val = lax.dynamic_slice(density, ((blocks[row_slot] * FB).astype(jnp.int32), (start_col * FB).astype(jnp.int32)), (FB, FB))
            col_parts.append(jnp.where(inside, block_val, jnp.zeros_like(block_val)))
        row_parts.append(jnp.concatenate(col_parts, axis=1))
    return jnp.concatenate(row_parts, axis=0)

def point_hidden(rho, in_weight, in_bias):
    return jax.nn.silu(rho[:, None] * in_weight[None, :] + in_bias[None, :]).astype(jnp.bfloat16)

def reference(basis_values, density, sig_blocks, grid_weights, atom_of, in_weight, in_bias, atom_proj, hidden_weight, atom_in, hidden_bias, out_weight):

    def first_pass(carry, inputs):
        sums_acc, squares_acc = carry
        values, blocks, weights, atoms = inputs
        sub = batch_density(density, blocks)
        mixed = jnp.dot(values, sub, preferred_element_type=jnp.float32)
        rho = lax.optimization_barrier(jnp.sum(mixed * values.astype(jnp.float32), axis=1))
        hidden = point_hidden(rho, in_weight, in_bias)
        proj = jnp.dot(hidden, atom_proj, preferred_element_type=jnp.float32)
        sums_acc = sums_acc + jax.ops.segment_sum(weights[:, None] * proj, atoms, num_segments=NATOM)
        squares_acc = squares_acc + jax.ops.segment_sum(weights * weights, atoms, num_segments=NATOM)
        return ((sums_acc, squares_acc), rho)
    start = (jnp.zeros((NATOM, ATW), jnp.float32), jnp.zeros((NATOM,), jnp.float32))
    (atom_sums, atom_squares), rho_all = lax.scan(first_pass, start, (basis_values, sig_blocks, grid_weights, atom_of))
    atom_feature = (atom_sums / jnp.sqrt(atom_squares + eps_atom)[:, None]).astype(jnp.bfloat16)

    def second_pass(total, inputs):
        values, blocks, weights, atoms, rho = inputs
        hidden = point_hidden(rho, in_weight, in_bias)
        near_feature = atom_feature[atoms]
        before = jnp.dot(hidden, hidden_weight, preferred_element_type=jnp.float32) + jnp.dot(near_feature, atom_in, preferred_element_type=jnp.float32) + hidden_bias[None, :]
        second = jax.nn.silu(before).astype(jnp.bfloat16)
        point_potential = jnp.dot(second, out_weight, preferred_element_type=jnp.float32)
        weighted = ((weights * point_potential)[:, None] * values.astype(jnp.float32)).astype(jnp.bfloat16)
        batch_matrix = lax.dot_general(values, weighted, (((0,), (0,)), ((), ())), preferred_element_type=jnp.float32)
        chip_of = blocks // CHIPB
        for row_slot in range(SIGB):
            for col_slot in range(SIGB):
                start_col = blocks[col_slot] - CHIPB * (chip_of[row_slot] - 1)
                inside = jnp.abs(chip_of[col_slot] - chip_of[row_slot]) <= 1
                start_col = jnp.clip(start_col, 0, 3 * CHIPB - 1)
                block_val = batch_matrix[row_slot * FB:(row_slot + 1) * FB, col_slot * FB:(col_slot + 1) * FB]
                block_val = jnp.where(inside, block_val, jnp.zeros_like(block_val))
                corner = ((blocks[row_slot] * FB).astype(jnp.int32), (start_col * FB).astype(jnp.int32))
                current = lax.dynamic_slice(total, corner, (FB, FB))
                total = lax.dynamic_update_slice(total, current + block_val, corner)
        return (total, None)
    potential, _ = lax.scan(second_pass, jnp.zeros((NFUNC, WINF), jnp.float32), (basis_values, sig_blocks, grid_weights, atom_of, rho_all))
    return potential
```

```python
import jax
import jax.numpy as jnp
from jax import lax
from jax.experimental import pallas as pl
from jax.experimental.pallas import tpu as pltpu
from jax.sharding import PartitionSpec as P

FB = 128
SIGB = 4
SIGF = 512
ATW = 64
HID = 256
CHIPB = 4
WINB = 12
HALF = 256
CHIPF = 512
CHIPA = 32
SEGS = 96
TILE = 2048
TRANS = 1024
MIB = 2**20
XROWS = 72

eps_atom = 0.0001
f32 = jnp.float32
bf16 = jnp.bfloat16

SMEM = pl.BlockSpec(memory_space=pltpu.SMEM)
VMEM = pl.BlockSpec(memory_space=pltpu.VMEM)
ANY = pl.BlockSpec(memory_space=pl.ANY)


def silu(v):
    h = 0.5 * v
    return h + h * jnp.tanh(h)


def block_of(i):
    return pl.ds(pl.multiple_of(i * FB, FB), FB)


def near(r, v):
    return jnp.abs(r // CHIPB - v // CHIPB) <= 1


def transpose_kernel(basis_ref, out_ref, token_ref):
    out_ref[0] = basis_ref[0].T
    token_ref[...] = jnp.zeros_like(token_ref)


def transpose_basis(basis):
    batches, points, funcs = basis.shape
    return pl.pallas_call(
        transpose_kernel,
        grid=(batches, points // TRANS),
        in_specs=[pl.BlockSpec((1, TRANS, funcs), lambda b, t: (b, t, 0))],
        out_specs=[
            pl.BlockSpec((1, funcs, TRANS), lambda b, t: (b, 0, t)),
            pl.BlockSpec((16, 128), lambda b, t: (0, 0)),
        ],
        out_shape=[
            jax.ShapeDtypeStruct((batches, funcs, points), bf16),
            jax.ShapeDtypeStruct((16, 128), bf16),
        ],
        compiler_params=pltpu.CompilerParams(vmem_limit_bytes=56 * MIB),
        cost_estimate=pl.CostEstimate(
            flops=10**10, bytes_accessed=4 * basis.size, transcendentals=0
        ),
    )(basis)


def tiles_of(points, batches):
    per = points // TILE
    return [(b, pl.ds(t * TILE, TILE)) for b in range(batches) for t in range(per)]


def fetch(src, dst, tiles, sems):
    copies = [
        pltpu.make_async_copy(src.at[b, :, cols], dst.at[b, :, cols], sems.at[i])
        for i, (b, cols) in enumerate(tiles)
    ]
    return copies


def first_kernel(
    scal_ref,
    own_ref,
    sib_ref,
    side_ref,
    side_sib_ref,
    bt_hbm,
    w_ref,
    atom_ref,
    in_w_ref,
    in_b_ref,
    proj_ref,
    hid_hbm,
    sums_ref,
    bt_ref,
    hid_ref,
    sub,
    acc,
    squares,
    bt_sems,
    hid_sems,
):
    core = scal_ref[8]
    atom_start = scal_ref[9]
    batches = bt_ref.shape[0]
    tiles = tiles_of(bt_ref.shape[2], batches)
    loads = fetch(bt_hbm, bt_ref, tiles, bt_sems)
    stores = fetch(hid_ref, hid_hbm, tiles, hid_sems)
    for load in loads:
        load.start()
    sources = (
        (0, side_ref, side_sib_ref, 0, 0),
        (1, own_ref, sib_ref, 0, 0),
        (2, side_ref, side_sib_ref, 2, CHIPB),
    )

    def place(i, _):
        b, k = i // SIGB, i % SIGB
        r = scal_ref[i]
        here = (r % CHIPB) // 2 == core
        for chip, mine, other, row, first in sources:
            for ref, held in ((mine, here), (other, jnp.logical_not(here))):

                @pl.when((r // CHIPB == chip) & held)
                def _():
                    for l in range(SIGB):
                        v = scal_ref[b * SIGB + l]
                        col = jnp.clip(v - first, 0, ref.shape[1] // FB - 1)
                        block = ref[block_of(row + r % 2), block_of(col)]
                        sub[b, block_of(k), l * FB : (l + 1) * FB] = jnp.where(
                            near(r, v), block, jnp.zeros_like(block)
                        )

        return 0

    lax.fori_loop(0, batches * SIGB, place, 0)
    acc[...] = jnp.zeros_like(acc)
    squares[...] = jnp.zeros_like(squares)

    def density_at(i):
        b, cols = tiles[i]
        loads[i].wait()
        bt = bt_ref[b, :, cols]
        mixed = jnp.dot(sub[b], bt, preferred_element_type=f32)
        return jnp.sum(mixed * bt.astype(f32), axis=0, keepdims=True)

    def gather_sums(i, rho):
        b, cols = tiles[i]
        hidden = silu(rho * in_w_ref[...] + in_b_ref[...]).astype(bf16)
        hid_ref[b, :, cols] = hidden
        stores[i].start()
        w = w_ref[b : b + 1, cols]
        atom = atom_ref[b : b + 1, cols] - atom_start
        w_high = w.astype(bf16).astype(f32)
        w_low = w - w_high
        match = lax.broadcasted_iota(jnp.int32, (SEGS, TILE), 0) == atom
        zero = jnp.zeros((SEGS, TILE), f32)
        member = jnp.concatenate(
            [jnp.where(match, w_high, zero), jnp.where(match, w_low, zero)], axis=0
        ).astype(bf16)
        acc[...] += lax.dot_general(
            hidden, member, (((1,), (1,)), ((), ())), preferred_element_type=f32
        )
        part = jnp.where(match, w * w, zero)
        total = part[:, :128]
        for j in range(1, TILE // 128):
            total = total + part[:, j * 128 : (j + 1) * 128]
        squares[...] += total

    rho = density_at(0)
    for i in range(1, len(tiles)):
        later = density_at(i)
        gather_sums(i - 1, rho)
        rho = later
    gather_sums(len(tiles) - 1, rho)
    weighted = acc[:, :SEGS] + acc[:, SEGS:]
    sums = jnp.dot(
        proj_ref[...].astype(f32).T,
        weighted,
        precision=lax.Precision.HIGHEST,
        preferred_element_type=f32,
    )
    sums_ref[...] = jnp.zeros_like(sums_ref)
    sums_ref[:ATW, :SEGS] = sums
    row = jnp.sum(squares[...].T, axis=0, keepdims=True)
    sums_ref[ATW : ATW + 1, :SEGS] = row
    for store in stores:
        store.wait()


def first_pass(scal, rows, bt, w, atom, in_w, in_b, proj):
    batches, funcs, points = bt.shape
    tiles = batches * points // TILE
    return pl.pallas_call(
        first_kernel,
        in_specs=[SMEM] + [VMEM] * 4 + [ANY] + [VMEM] * 5,
        out_specs=[ANY, VMEM],
        out_shape=[
            jax.ShapeDtypeStruct((batches, HID, points), bf16),
            jax.ShapeDtypeStruct((XROWS, 128), f32),
        ],
        scratch_shapes=[
            pltpu.VMEM(bt.shape, bf16),
            pltpu.VMEM((batches, HID, points), bf16),
            pltpu.VMEM((batches, SIGF, SIGF), bf16),
            pltpu.VMEM((HID, 2 * SEGS), f32),
            pltpu.VMEM((SEGS, 128), f32),
            pltpu.SemaphoreType.DMA((tiles,)),
            pltpu.SemaphoreType.DMA((tiles,)),
        ],
        compiler_params=pltpu.CompilerParams(vmem_limit_bytes=52 * MIB),
    )(scal, *rows, bt, w, atom, in_w, in_b, proj)


def second_kernel(
    scal_ref,
    x_ref,
    l1_ref,
    l2_ref,
    r1_ref,
    r2_ref,
    atom_in_ref,
    hw_ref,
    hb_ref,
    ow_ref,
    w_ref,
    atom_ref,
    hid_hbm,
    bt_hbm,
    mats_ref,
    hid_ref,
    bt_ref,
    hw_t,
    feature,
    hid_sems,
    bt_sems,
):
    atom_start = scal_ref[9]
    tiles = tiles_of(bt_ref.shape[2], bt_ref.shape[0])
    hid_loads = fetch(hid_hbm, hid_ref, tiles, hid_sems)
    bt_loads = fetch(bt_hbm, bt_ref, tiles, bt_sems)
    for hid_load, bt_load in zip(hid_loads, bt_loads):
        hid_load.start()
        bt_load.start()

    def part(ref, start, size):
        return ref[:, start * CHIPA : (start + size) * CHIPA]

    zero = jnp.zeros((XROWS, 2 * CHIPA), f32)
    total = x_ref[:, :SEGS]
    total = total + jnp.concatenate([part(l1_ref, 1, 2), zero[:, :CHIPA]], axis=1)
    total = total + jnp.concatenate([part(l2_ref, 2, 1), zero], axis=1)
    total = total + jnp.concatenate([zero[:, :CHIPA], part(r1_ref, 0, 2)], axis=1)
    total = total + jnp.concatenate([zero, part(r2_ref, 0, 1)], axis=1)
    scaled = total[:ATW] / jnp.sqrt(total[ATW : ATW + 1] + eps_atom)
    value = jnp.dot(
        atom_in_ref[...].T, scaled.astype(bf16), preferred_element_type=f32
    )
    high = value.astype(bf16)
    low = (value - high.astype(f32)).astype(bf16)
    feature[...] = jnp.concatenate([high, low], axis=1)
    hw_t[...] = hw_ref[...].T
    mats_ref[...] = jnp.zeros_like(mats_ref)

    def weigh(i):
        b, cols = tiles[i]
        atom = atom_ref[b : b + 1, cols] - atom_start
        ids = lax.broadcasted_iota(jnp.int32, (SEGS, TILE), 0)
        match = (ids == atom).astype(f32)
        member = jnp.concatenate([match, match], axis=0).astype(bf16)
        hid_loads[i].wait()
        before = (
            jnp.dot(hw_t[...], hid_ref[b, :, cols], preferred_element_type=f32)
            + jnp.dot(feature[...], member, preferred_element_type=f32)
            + hb_ref[...]
        )
        second = silu(before).astype(bf16).astype(f32)
        point = jnp.sum(second * ow_ref[...], axis=0, keepdims=True)
        scale = w_ref[b : b + 1, cols] * point
        bt_loads[i].wait()
        return (bt_ref[b, :, cols].astype(f32) * scale).astype(bf16)

    def gram(i, weighted):
        b, cols = tiles[i]
        mats_ref[b] += lax.dot_general(
            bt_ref[b, :, cols],
            weighted,
            (((1,), (1,)), ((), ())),
            preferred_element_type=f32,
        )

    weighted = weigh(0)
    for i in range(1, len(tiles)):
        later = weigh(i)
        gram(i - 1, weighted)
        weighted = later
    gram(len(tiles) - 1, weighted)


def second_pass(scal, sums, atom_in, hw, hb, ow, w, atom, hid, bt):
    batches, funcs, points = bt.shape
    tiles = batches * points // TILE
    return pl.pallas_call(
        second_kernel,
        in_specs=[SMEM] + [VMEM] * 11 + [ANY] * 2,
        out_specs=VMEM,
        out_shape=jax.ShapeDtypeStruct((batches, SIGF, SIGF), f32),
        scratch_shapes=[
            pltpu.VMEM(hid.shape, bf16),
            pltpu.VMEM(bt.shape, bf16),
            pltpu.VMEM((HID, HID), bf16),
            pltpu.VMEM((HID, 2 * SEGS), bf16),
            pltpu.SemaphoreType.DMA((tiles,)),
            pltpu.SemaphoreType.DMA((tiles,)),
        ],
        compiler_params=pltpu.CompilerParams(vmem_limit_bytes=52 * MIB),
    )(scal, *sums, atom_in, hw, hb, ow, w, atom, hid, bt)


def side_kernel(
    scal_ref, other_ref, mats_ref, got_ref, left_ref, own_ref, right_ref, to_left, to_right
):
    core = scal_ref[8]
    to_left[...] = jnp.zeros_like(to_left)
    to_right[...] = jnp.zeros_like(to_right)
    own_ref[...] = jnp.zeros_like(own_ref)
    targets = ((0, to_left, 0), (1, own_ref, 0), (2, to_right, CHIPB))
    for blocks_ref, source in ((scal_ref, mats_ref), (other_ref, got_ref)):

        def place(i, _):
            b, k = i // SIGB, i % SIGB
            r = blocks_ref[i]
            here = (r % CHIPB) // 2 == core
            for chip, ref, first in targets:

                @pl.when((r // CHIPB == chip) & here)
                def _():
                    rows = block_of(r % 2)
                    for l in range(SIGB):
                        v = blocks_ref[b * SIGB + l]
                        cols = block_of(jnp.clip(v - first, 0, ref.shape[1] // FB - 1))
                        block = source[b, block_of(k), l * FB : (l + 1) * FB]
                        ref[rows, cols] = ref[rows, cols] + jnp.where(
                            near(r, v), block, jnp.zeros_like(block)
                        )

            return 0

        lax.fori_loop(0, source.shape[0] * SIGB, place, 0)
    left_ref[...] = to_left[...].astype(bf16)
    right_ref[...] = to_right[...].astype(bf16)


def side_sums(scal, other, mats, got):
    side = jax.ShapeDtypeStruct((HALF, 2 * CHIPF), bf16)
    return pl.pallas_call(
        side_kernel,
        in_specs=[SMEM, SMEM, VMEM, VMEM],
        out_specs=[VMEM] * 3,
        out_shape=[side, jax.ShapeDtypeStruct((HALF, 3 * CHIPF), f32), side],
        scratch_shapes=[pltpu.VMEM((HALF, 2 * CHIPF), f32)] * 2,
        compiler_params=pltpu.CompilerParams(vmem_limit_bytes=20 * MIB),
    )(scal, other, mats, got)


def final_kernel(own_ref, left_ref, right_ref, out_ref):
    chip = CHIPF
    out_ref[:, :chip] = own_ref[:, :chip] + left_ref[:, :chip].astype(f32)
    out_ref[:, chip : 2 * chip] = (
        own_ref[:, chip : 2 * chip]
        + left_ref[:, chip:].astype(f32)
        + right_ref[:, :chip].astype(f32)
    )
    out_ref[:, 2 * chip :] = own_ref[:, 2 * chip :] + right_ref[:, chip:].astype(f32)


def final_sum(own, left, right):
    rows, cols = own.shape
    strip = 64
    wide = pl.BlockSpec((strip, cols), lambda i: (i, 0))
    side = pl.BlockSpec((strip, 2 * CHIPF), lambda i: (i, 0))
    return pl.pallas_call(
        final_kernel,
        grid=(rows // strip,),
        in_specs=[wide, side, side],
        out_specs=wide,
        out_shape=jax.ShapeDtypeStruct((rows, cols), f32),
        compiler_params=pltpu.CompilerParams(vmem_limit_bytes=12 * MIB),
    )(own, left, right)


def on_device(
    basis_values,
    density,
    sig_blocks,
    grid_weights,
    atom_of,
    in_weight,
    in_bias,
    atom_proj,
    hidden_weight,
    atom_in,
    hidden_bias,
    out_weight,
):
    chips = lax.axis_size("pts")
    chip = lax.axis_index("pts")
    core = lax.axis_index("blk")

    def shift(x, by):
        return lax.ppermute(x, "pts", [(i, (i + by) % chips) for i in range(chips)])

    def swap(x):
        return lax.ppermute(x, "blk", [(0, 1), (1, 0)])

    scal = jnp.concatenate(
        [
            (sig_blocks - CHIPB * (chip - 1)).reshape(-1),
            core[None].astype(jnp.int32),
            (CHIPA * (chip - 1))[None].astype(jnp.int32),
        ]
    )
    from_left = shift(density[:, CHIPF:], 1)
    from_right = shift(density[:, : 2 * CHIPF], -1)
    sibling = swap(density)
    other = swap(scal)
    bt, token = transpose_basis(basis_values)
    side = jnp.concatenate([from_left, from_right], axis=0) + token[0, 0]
    side_sib = swap(side)

    column = lambda x: x.astype(f32).reshape(HID, 1)
    hidden, sums = first_pass(
        scal,
        (density, sibling, side, side_sib),
        bt,
        grid_weights,
        atom_of,
        column(in_weight),
        column(in_bias),
        atom_proj,
    )
    sums = sums + swap(sums)
    near_sums = [shift(sums, by) for by in (1, 2, -1, -2)]
    mats = second_pass(
        scal,
        [sums] + near_sums,
        atom_in,
        hidden_weight,
        column(hidden_bias),
        column(out_weight),
        grid_weights,
        atom_of,
        hidden,
        bt,
    )
    to_left, own, to_right = side_sums(scal, other, mats, swap(mats))
    return final_sum(own, shift(to_right, 1), shift(to_left, -1))


def solution(mesh):
    return jax.shard_map(
        on_device,
        mesh=mesh,
        in_specs=(
            P(("pts", "blk"), None, None),
            P(("pts", "blk"), None),
            P(("pts", "blk"), None),
            P(("pts", "blk"), None),
            P(("pts", "blk"), None),
            P(),
            P(),
            P(),
            P(),
            P(),
            P(),
            P(),
        ),
        out_specs=P(("pts", "blk"), None),
        check_vma=False,
    )
```

```python
import jax
import jax.numpy as jnp
from jax import lax
from jax.experimental import pallas as pl
from jax.experimental.pallas import tpu as pltpu
from jax.sharding import PartitionSpec as P

FB = 128
SIGB = 4
SIGF = 512
ATW = 64
HID = 256
CHIPB = 4
WINB = 12
HALF = 256
CHIPF = 512
CHIPA = 32
SEGS = 96
TILE = 2048
TRANS = 1024
MIB = 2**20
XROWS = 72

eps_atom = 0.0001
f32 = jnp.float32
bf16 = jnp.bfloat16

SMEM = pl.BlockSpec(memory_space=pltpu.SMEM)
VMEM = pl.BlockSpec(memory_space=pltpu.VMEM)
ANY = pl.BlockSpec(memory_space=pl.ANY)


def silu_of_twice(h):
    return h * (1.0 + jnp.tanh(h))


def block_of(i):
    return pl.ds(pl.multiple_of(i * FB, FB), FB)


def near(r, v):
    return jnp.abs(r // CHIPB - v // CHIPB) <= 1


def transpose_kernel(basis_ref, out_ref, token_ref):
    out_ref[0] = basis_ref[0].T
    token_ref[...] = jnp.zeros_like(token_ref)


def transpose_basis(basis):
    batches, points, funcs = basis.shape
    return pl.pallas_call(
        transpose_kernel,
        grid=(batches, points // TRANS),
        in_specs=[pl.BlockSpec((1, TRANS, funcs), lambda b, t: (b, t, 0))],
        out_specs=[
            pl.BlockSpec((1, funcs, TRANS), lambda b, t: (b, 0, t)),
            pl.BlockSpec((16, 128), lambda b, t: (0, 0)),
        ],
        out_shape=[
            jax.ShapeDtypeStruct((batches, funcs, points), bf16),
            jax.ShapeDtypeStruct((16, 128), bf16),
        ],
        compiler_params=pltpu.CompilerParams(vmem_limit_bytes=56 * MIB),
        cost_estimate=pl.CostEstimate(
            flops=10**10, bytes_accessed=4 * basis.size, transcendentals=0
        ),
    )(basis)


def tiles_of(points, batches):
    per = points // TILE
    return [(b, pl.ds(t * TILE, TILE)) for b in range(batches) for t in range(per)]


def fetch(src, dst, tiles, sems):
    copies = [
        pltpu.make_async_copy(src.at[b, :, cols], dst.at[b, :, cols], sems.at[i])
        for i, (b, cols) in enumerate(tiles)
    ]
    return copies


def first_kernel(
    scal_ref,
    own_ref,
    sib_ref,
    side_ref,
    side_sib_ref,
    bt_hbm,
    w_ref,
    atom_ref,
    in_w_ref,
    in_b_ref,
    proj_ref,
    hid_hbm,
    sums_ref,
    bt_ref,
    hid_ref,
    sub,
    acc,
    squares,
    bt_sems,
    hid_sems,
):
    core = scal_ref[8]
    atom_start = scal_ref[9]
    batches = bt_ref.shape[0]
    tiles = tiles_of(bt_ref.shape[2], batches)
    loads = fetch(bt_hbm, bt_ref, tiles, bt_sems)
    stores = fetch(hid_ref, hid_hbm, tiles, hid_sems)
    for load in loads:
        load.start()
    sources = (
        (0, side_ref, side_sib_ref, 0, 0),
        (1, own_ref, sib_ref, 0, 0),
        (2, side_ref, side_sib_ref, 2, CHIPB),
    )

    def place(i, _):
        b, k = i // SIGB, i % SIGB
        r = scal_ref[i]
        here = (r % CHIPB) // 2 == core
        for chip, mine, other, row, first in sources:
            for ref, held in ((mine, here), (other, jnp.logical_not(here))):

                @pl.when((r // CHIPB == chip) & held)
                def _():
                    for l in range(SIGB):
                        v = scal_ref[b * SIGB + l]
                        col = jnp.clip(v - first, 0, ref.shape[1] // FB - 1)
                        block = ref[block_of(row + r % 2), block_of(col)]
                        sub[b, block_of(k), l * FB : (l + 1) * FB] = jnp.where(
                            near(r, v), block, jnp.zeros_like(block)
                        )

        return 0

    lax.fori_loop(0, batches * SIGB, place, 0)
    acc[...] = jnp.zeros_like(acc)
    squares[...] = jnp.zeros_like(squares)

    def density_at(i):
        b, cols = tiles[i]
        loads[i].wait()
        bt = bt_ref[b, :, cols]
        mixed = jnp.dot(sub[b], bt, preferred_element_type=f32)
        return jnp.sum(mixed * bt.astype(f32), axis=0, keepdims=True)

    def gather_sums(i, rho):
        b, cols = tiles[i]
        hidden = silu_of_twice(rho * in_w_ref[...] + in_b_ref[...]).astype(bf16)
        hid_ref[b, :, cols] = hidden
        stores[i].start()
        w = w_ref[b : b + 1, cols]
        atom = atom_ref[b : b + 1, cols] - atom_start
        w_high = w.astype(bf16).astype(f32)
        w_low = w - w_high
        match = lax.broadcasted_iota(jnp.int32, (SEGS, TILE), 0) == atom
        zero = jnp.zeros((SEGS, TILE), f32)
        member = jnp.concatenate(
            [jnp.where(match, w_high, zero), jnp.where(match, w_low, zero)], axis=0
        ).astype(bf16)
        acc[...] += lax.dot_general(
            hidden, member, (((1,), (1,)), ((), ())), preferred_element_type=f32
        )
        part = jnp.where(match, w * w, zero)
        total = part[:, :128]
        for j in range(1, TILE // 128):
            total = total + part[:, j * 128 : (j + 1) * 128]
        squares[...] += total

    for i in range(len(tiles)):
        gather_sums(i, density_at(i))
    weighted = acc[:, :SEGS] + acc[:, SEGS:]
    sums = jnp.dot(
        proj_ref[...].astype(f32).T,
        weighted,
        precision=lax.Precision.HIGHEST,
        preferred_element_type=f32,
    )
    sums_ref[...] = jnp.zeros_like(sums_ref)
    sums_ref[:ATW, :SEGS] = sums
    row = jnp.sum(squares[...].T, axis=0, keepdims=True)
    sums_ref[ATW : ATW + 1, :SEGS] = row
    for store in stores:
        store.wait()


def first_pass(scal, rows, bt, w, atom, in_w, in_b, proj):
    batches, funcs, points = bt.shape
    tiles = batches * points // TILE
    return pl.pallas_call(
        first_kernel,
        in_specs=[SMEM] + [VMEM] * 4 + [ANY] + [VMEM] * 5,
        out_specs=[ANY, VMEM],
        out_shape=[
            jax.ShapeDtypeStruct((batches, HID, points), bf16),
            jax.ShapeDtypeStruct((XROWS, 128), f32),
        ],
        scratch_shapes=[
            pltpu.VMEM(bt.shape, bf16),
            pltpu.VMEM((batches, HID, points), bf16),
            pltpu.VMEM((batches, SIGF, SIGF), bf16),
            pltpu.VMEM((HID, 2 * SEGS), f32),
            pltpu.VMEM((SEGS, 128), f32),
            pltpu.SemaphoreType.DMA((tiles,)),
            pltpu.SemaphoreType.DMA((tiles,)),
        ],
        compiler_params=pltpu.CompilerParams(vmem_limit_bytes=52 * MIB),
    )(scal, *rows, bt, w, atom, in_w, in_b, proj)


def layer_kernel(hw_ref, hid_ref, out_ref, hw_t):
    @pl.when((pl.program_id(0) == 0) & (pl.program_id(1) == 0))
    def _():
        hw_t[...] = (0.5 * hw_ref[...].astype(f32)).T.astype(bf16)

    out_ref[0] = jnp.dot(hw_t[...], hid_ref[0], preferred_element_type=f32)


def layer(hw, hid):
    batches, units, points = hid.shape
    spec = pl.BlockSpec((1, units, TILE), lambda b, t: (b, 0, t))
    return pl.pallas_call(
        layer_kernel,
        grid=(batches, points // TILE),
        in_specs=[pl.BlockSpec((units, units), lambda b, t: (0, 0)), spec],
        out_specs=spec,
        out_shape=jax.ShapeDtypeStruct(hid.shape, f32),
        scratch_shapes=[pltpu.VMEM((units, units), bf16)],
        compiler_params=pltpu.CompilerParams(vmem_limit_bytes=52 * MIB),
        cost_estimate=pl.CostEstimate(
            flops=10**10, bytes_accessed=6 * hid.size, transcendentals=0
        ),
    )(hw, hid)


def second_kernel(
    scal_ref,
    x_ref,
    even_ref,
    odd_ref,
    even2_ref,
    odd2_ref,
    atom_in_ref,
    hb_ref,
    ow_ref,
    w_ref,
    atom_ref,
    hid_hbm,
    bt_hbm,
    mats_ref,
    send_ref,
    hid_ref,
    bt_ref,
    feature,
    hid_sems,
    bt_sems,
):
    atom_start = scal_ref[9]
    tiles = tiles_of(bt_ref.shape[2], bt_ref.shape[0])
    hid_loads = fetch(hid_hbm, hid_ref, tiles, hid_sems)
    bt_loads = fetch(bt_hbm, bt_ref, tiles, bt_sems)
    for hid_load, bt_load in zip(hid_loads, bt_loads):
        hid_load.start()
        bt_load.start()

    first = scal_ref[10] == 0
    first2 = scal_ref[11] == 0
    left1 = jnp.where(first, odd_ref[...], even_ref[...])
    right1 = jnp.where(first, even_ref[...], odd_ref[...])
    left2 = jnp.where(first2, odd2_ref[...], even2_ref[...])
    right2 = jnp.where(first2, even2_ref[...], odd2_ref[...])

    def part(x, start, size):
        return x[:, start * CHIPA : (start + size) * CHIPA]

    zero = jnp.zeros((XROWS, 2 * CHIPA), f32)
    total = x_ref[:, :SEGS]
    total = total + jnp.concatenate([part(left1, 1, 2), zero[:, :CHIPA]], axis=1)
    total = total + jnp.concatenate([part(left2, 2, 1), zero], axis=1)
    total = total + jnp.concatenate([zero[:, :CHIPA], part(right1, 0, 2)], axis=1)
    total = total + jnp.concatenate([zero, part(right2, 0, 1)], axis=1)
    scaled = total[:ATW] / jnp.sqrt(total[ATW : ATW + 1] + eps_atom)
    value = jnp.dot(
        atom_in_ref[...].T, scaled.astype(bf16), preferred_element_type=f32
    )
    value = 0.5 * (value + hb_ref[...])
    high = value.astype(bf16)
    low = (value - high.astype(f32)).astype(bf16)
    feature[...] = jnp.concatenate([high, low], axis=1)
    mats_ref[...] = jnp.zeros_like(mats_ref)

    def weigh(i):
        b, cols = tiles[i]
        atom = atom_ref[b : b + 1, cols] - atom_start
        ids = lax.broadcasted_iota(jnp.int32, (SEGS, TILE), 0)
        match = (ids == atom).astype(f32)
        member = jnp.concatenate([match, match], axis=0).astype(bf16)
        hid_loads[i].wait()
        half = hid_ref[b, :, cols] + jnp.dot(
            feature[...], member, preferred_element_type=f32
        )
        second = silu_of_twice(half)
        point = jnp.sum(second * ow_ref[...], axis=0, keepdims=True)
        scale = w_ref[b : b + 1, cols] * point
        bt_loads[i].wait()
        return (bt_ref[b, :, cols].astype(f32) * scale).astype(bf16)

    def gram(i, weighted):
        b, cols = tiles[i]
        mats_ref[b] += lax.dot_general(
            bt_ref[b, :, cols],
            weighted,
            (((1,), (1,)), ((), ())),
            preferred_element_type=f32,
        )

    for i in range(len(tiles)):
        gram(i, weigh(i))
    send_ref[...] = mats_ref[...].astype(bf16)


def second_pass(scal, sums, atom_in, hb, ow, w, atom, hid, bt):
    batches, funcs, points = bt.shape
    tiles = batches * points // TILE
    return pl.pallas_call(
        second_kernel,
        in_specs=[SMEM] + [VMEM] * 10 + [ANY] * 2,
        out_specs=[VMEM] * 2,
        out_shape=[
            jax.ShapeDtypeStruct((batches, SIGF, SIGF), f32),
            jax.ShapeDtypeStruct((batches, SIGF, SIGF), bf16),
        ],
        scratch_shapes=[
            pltpu.VMEM(hid.shape, f32),
            pltpu.VMEM(bt.shape, bf16),
            pltpu.VMEM((HID, 2 * SEGS), bf16),
            pltpu.SemaphoreType.DMA((tiles,)),
            pltpu.SemaphoreType.DMA((tiles,)),
        ],
        compiler_params=pltpu.CompilerParams(vmem_limit_bytes=52 * MIB),
    )(scal, *sums, atom_in, hb, ow, w, atom, hid, bt)


def scatter(scal_ref, other_ref, mats_ref, got_ref, targets):
    core = scal_ref[8]
    for _, ref, _ in targets:
        ref[...] = jnp.zeros_like(ref)
    for blocks_ref, source in ((scal_ref, mats_ref), (other_ref, got_ref)):

        def place(i, _):
            b, k = i // SIGB, i % SIGB
            r = blocks_ref[i]
            here = (r % CHIPB) // 2 == core
            for chip, ref, first in targets:

                @pl.when((r // CHIPB == chip) & here)
                def _():
                    rows = block_of(r % 2)
                    for l in range(SIGB):
                        v = blocks_ref[b * SIGB + l]
                        cols = block_of(jnp.clip(v - first, 0, ref.shape[1] // FB - 1))
                        block = source[b, block_of(k), l * FB : (l + 1) * FB].astype(f32)
                        ref[rows, cols] = ref[rows, cols] + jnp.where(
                            near(r, v), block, jnp.zeros_like(block)
                        )

            return 0

        lax.fori_loop(0, source.shape[0] * SIGB, place, 0)


def side_kernel(
    scal_ref, other_ref, mats_ref, got_ref, left_ref, right_ref, to_left, to_right
):
    targets = ((0, to_left, 0), (2, to_right, CHIPB))
    scatter(scal_ref, other_ref, mats_ref, got_ref, targets)
    left_ref[...] = to_left[...].astype(bf16)
    right_ref[...] = to_right[...].astype(bf16)


def side_sums(scal, other, mats, got):
    side = jax.ShapeDtypeStruct((HALF, 2 * CHIPF), bf16)
    return pl.pallas_call(
        side_kernel,
        in_specs=[SMEM, SMEM, VMEM, VMEM],
        out_specs=[VMEM] * 2,
        out_shape=[side] * 2,
        scratch_shapes=[pltpu.VMEM((HALF, 2 * CHIPF), f32)] * 2,
        compiler_params=pltpu.CompilerParams(vmem_limit_bytes=20 * MIB),
    )(scal, other, mats, got)


def own_kernel(scal_ref, other_ref, mats_ref, got_ref, own_ref):
    scatter(scal_ref, other_ref, mats_ref, got_ref, ((1, own_ref, 0),))


def own_sums(scal, other, mats, got):
    return pl.pallas_call(
        own_kernel,
        in_specs=[SMEM, SMEM, VMEM, VMEM],
        out_specs=VMEM,
        out_shape=jax.ShapeDtypeStruct((HALF, 3 * CHIPF), f32),
        compiler_params=pltpu.CompilerParams(vmem_limit_bytes=20 * MIB),
        cost_estimate=pl.CostEstimate(
            flops=10**9, bytes_accessed=8 * mats.size, transcendentals=0
        ),
    )(scal, other, mats, got)


def final_kernel(own_ref, left_ref, right_ref, out_ref):
    chip = CHIPF
    out_ref[:, :chip] = own_ref[:, :chip] + left_ref[:, :chip].astype(f32)
    out_ref[:, chip : 2 * chip] = (
        own_ref[:, chip : 2 * chip]
        + left_ref[:, chip:].astype(f32)
        + right_ref[:, :chip].astype(f32)
    )
    out_ref[:, 2 * chip :] = own_ref[:, 2 * chip :] + right_ref[:, chip:].astype(f32)


def final_sum(own, left, right):
    rows, cols = own.shape
    strip = 128
    wide = pl.BlockSpec((strip, cols), lambda i: (i, 0))
    side = pl.BlockSpec((strip, 2 * CHIPF), lambda i: (i, 0))
    return pl.pallas_call(
        final_kernel,
        grid=(rows // strip,),
        in_specs=[wide, side, side],
        out_specs=wide,
        out_shape=jax.ShapeDtypeStruct((rows, cols), f32),
        compiler_params=pltpu.CompilerParams(vmem_limit_bytes=12 * MIB),
    )(own, left, right)


def on_device(
    basis_values,
    density,
    sig_blocks,
    grid_weights,
    atom_of,
    in_weight,
    in_bias,
    atom_proj,
    hidden_weight,
    atom_in,
    hidden_bias,
    out_weight,
):
    chips = lax.axis_size("pts")
    chip = lax.axis_index("pts")
    core = lax.axis_index("blk")

    def shift(x, by):
        return lax.ppermute(x, "pts", [(i, (i + by) % chips) for i in range(chips)])

    def pair(x, by, start):
        to = lambda i: (((i - start) % chips) ^ by) + start
        return lax.ppermute(x, "pts", [(i, to(i) % chips) for i in range(chips)])

    def swap(x):
        return lax.ppermute(x, "blk", [(0, 1), (1, 0)])

    scal = jnp.concatenate(
        [
            (sig_blocks - CHIPB * (chip - 1)).reshape(-1),
            core[None].astype(jnp.int32),
            (CHIPA * (chip - 1))[None].astype(jnp.int32),
            (chip % 2)[None].astype(jnp.int32),
            ((chip // 2) % 2)[None].astype(jnp.int32),
        ]
    )
    from_left = shift(density[:, CHIPF:], 1)
    from_right = shift(density[:, : 2 * CHIPF], -1)
    sibling = swap(density)
    other = swap(scal)
    bt, token = transpose_basis(basis_values)
    side = jnp.concatenate([from_left, from_right], axis=0) + token[0, 0]
    side_sib = swap(side)

    column = lambda x, by=1.0: (by * x.astype(f32)).reshape(HID, 1)
    hidden, sums = first_pass(
        scal,
        (density, sibling, side, side_sib),
        bt,
        grid_weights,
        atom_of,
        column(in_weight, 0.5),
        column(in_bias, 0.5),
        atom_proj,
    )
    sums = sums + swap(sums)
    near_sums = [pair(sums, by, start) for by, start in ((1, 0), (2, 0), (1, 1), (2, 2))]
    half = layer(hidden_weight, hidden)
    mats, send = second_pass(
        scal,
        [sums, near_sums[0], near_sums[2], near_sums[1], near_sums[3]],
        atom_in,
        column(hidden_bias),
        column(out_weight),
        grid_weights,
        atom_of,
        half,
        bt,
    )
    got = swap(send)
    to_left, to_right = side_sums(scal, other, mats, got)
    own = own_sums(scal, other, mats, got)
    return final_sum(own, shift(to_right, 1), shift(to_left, -1))


def solution(mesh):
    return jax.shard_map(
        on_device,
        mesh=mesh,
        in_specs=(
            P(("pts", "blk"), None, None),
            P(("pts", "blk"), None),
            P(("pts", "blk"), None),
            P(("pts", "blk"), None),
            P(("pts", "blk"), None),
            P(),
            P(),
            P(),
            P(),
            P(),
            P(),
            P(),
        ),
        out_specs=P(("pts", "blk"), None),
        check_vma=False,
    )
```

```python
import jax
import jax.numpy as jnp
from jax import lax
from jax.experimental import pallas as pl
from jax.experimental.pallas import tpu as pltpu
from jax.sharding import PartitionSpec as P

FB = 128
SIGB = 4
SIGF = 512
ATW = 64
HID = 256
CHIPB = 4
WINB = 12
HALF = 256
CHIPF = 512
CHIPA = 32
SEGS = 96
TILE = 2048
FIRST = (1024, 1024)
TRANS = 1024
MIB = 2**20
XROWS = 72

eps_atom = 0.0001
f32 = jnp.float32
bf16 = jnp.bfloat16

SMEM = pl.BlockSpec(memory_space=pltpu.SMEM)
VMEM = pl.BlockSpec(memory_space=pltpu.VMEM)
ANY = pl.BlockSpec(memory_space=pl.ANY)


def silu_of_twice(h):
    return h * (1.0 + jnp.tanh(h))


def block_of(i):
    return pl.ds(pl.multiple_of(i * FB, FB), FB)


def near(r, v):
    return jnp.abs(r // CHIPB - v // CHIPB) <= 1


def transpose_kernel(basis_ref, out_ref, token_ref):
    out_ref[0] = basis_ref[0].T
    token_ref[...] = jnp.zeros_like(token_ref)


def transpose_basis(basis):
    batches, points, funcs = basis.shape
    return pl.pallas_call(
        transpose_kernel,
        grid=(batches, points // TRANS),
        in_specs=[pl.BlockSpec((1, TRANS, funcs), lambda b, t: (b, t, 0))],
        out_specs=[
            pl.BlockSpec((1, funcs, TRANS), lambda b, t: (b, 0, t)),
            pl.BlockSpec((1, 2 * CHIPF), lambda b, t: (0, 0)),
        ],
        out_shape=[
            jax.ShapeDtypeStruct((batches, funcs, points), bf16),
            jax.ShapeDtypeStruct((1, 2 * CHIPF), bf16),
        ],
        compiler_params=pltpu.CompilerParams(vmem_limit_bytes=56 * MIB),
        cost_estimate=pl.CostEstimate(
            flops=10**10, bytes_accessed=4 * basis.size, transcendentals=0
        ),
    )(basis)


def tiles_of(points, batches):
    sizes = [[TILE] * (points // TILE) for _ in range(batches)]
    sizes[0] = list(FIRST) + sizes[0][1:]
    return [
        (b, pl.ds(sum(row[:i]), row[i])) for b, row in enumerate(sizes) for i in range(len(row))
    ]


def fetch(src, dst, tiles, sems):
    copies = [
        pltpu.make_async_copy(src.at[b, :, cols], dst.at[b, :, cols], sems.at[i])
        for i, (b, cols) in enumerate(tiles)
    ]
    return copies


def first_kernel(
    scal_ref,
    own_ref,
    sib_ref,
    side_ref,
    side_sib_ref,
    bt_hbm,
    w_ref,
    atom_ref,
    in_w_ref,
    in_b_ref,
    proj_ref,
    hid_hbm,
    sums_ref,
    bt_ref,
    hid_ref,
    sub,
    acc,
    squares,
    bt_sems,
    hid_sems,
):
    core = scal_ref[8]
    atom_start = scal_ref[9]
    batches = bt_ref.shape[0]
    tiles = tiles_of(bt_ref.shape[2], batches)
    loads = fetch(bt_hbm, bt_ref, tiles, bt_sems)
    stores = fetch(hid_ref, hid_hbm, tiles, hid_sems)
    for load in loads:
        load.start()
    sources = (
        (0, side_ref, side_sib_ref, 0, 0),
        (1, own_ref, sib_ref, 0, 0),
        (2, side_ref, side_sib_ref, 2, CHIPB),
    )

    def place(i, _):
        b, k = i // SIGB, i % SIGB
        r = scal_ref[i]
        here = (r % CHIPB) // 2 == core
        for chip, mine, other, row, first in sources:
            for ref, held in ((mine, here), (other, jnp.logical_not(here))):

                @pl.when((r // CHIPB == chip) & held)
                def _():
                    for l in range(SIGB):
                        v = scal_ref[b * SIGB + l]
                        col = jnp.clip(v - first, 0, ref.shape[1] // FB - 1)
                        block = ref[block_of(row + r % 2), block_of(col)]
                        sub[b, block_of(k), l * FB : (l + 1) * FB] = jnp.where(
                            near(r, v), block, jnp.zeros_like(block)
                        )

        return 0

    lax.fori_loop(0, batches * SIGB, place, 0)
    acc[...] = jnp.zeros_like(acc)
    squares[...] = jnp.zeros_like(squares)

    def density_at(i):
        b, cols = tiles[i]
        loads[i].wait()
        bt = bt_ref[b, :, cols]
        mixed = jnp.dot(sub[b], bt, preferred_element_type=f32)
        return jnp.sum(mixed * bt.astype(f32), axis=0, keepdims=True)

    def gather_sums(i, rho):
        b, cols = tiles[i]
        hidden = silu_of_twice(rho * in_w_ref[...] + in_b_ref[...]).astype(bf16)
        hid_ref[b, :, cols] = hidden
        stores[i].start()
        w = w_ref[b : b + 1, cols]
        atom = atom_ref[b : b + 1, cols] - atom_start
        w_high = w.astype(bf16).astype(f32)
        w_low = w - w_high
        match = lax.broadcasted_iota(jnp.int32, (SEGS, cols.size), 0) == atom
        zero = jnp.zeros((SEGS, cols.size), f32)
        member = jnp.concatenate(
            [jnp.where(match, w_high, zero), jnp.where(match, w_low, zero)], axis=0
        ).astype(bf16)
        acc[...] += lax.dot_general(
            hidden, member, (((1,), (1,)), ((), ())), preferred_element_type=f32
        )
        part = jnp.where(match, w * w, zero)
        total = part[:, :128]
        for j in range(1, cols.size // 128):
            total = total + part[:, j * 128 : (j + 1) * 128]
        squares[...] += total

    for i in range(len(tiles)):
        gather_sums(i, density_at(i))
    weighted = acc[:, :SEGS] + acc[:, SEGS:]
    sums = jnp.dot(
        proj_ref[...].astype(f32).T,
        weighted,
        precision=lax.Precision.HIGHEST,
        preferred_element_type=f32,
    )
    sums_ref[...] = jnp.zeros_like(sums_ref)
    sums_ref[:ATW, :SEGS] = sums
    row = jnp.sum(squares[...].T, axis=0, keepdims=True)
    sums_ref[ATW : ATW + 1, :SEGS] = row
    for store in stores:
        store.wait()


def first_pass(scal, rows, bt, w, atom, in_w, in_b, proj):
    batches, funcs, points = bt.shape
    tiles = len(tiles_of(points, batches))
    return pl.pallas_call(
        first_kernel,
        in_specs=[SMEM] + [VMEM] * 4 + [ANY] + [VMEM] * 5,
        out_specs=[ANY, VMEM],
        out_shape=[
            jax.ShapeDtypeStruct((batches, HID, points), bf16),
            jax.ShapeDtypeStruct((XROWS, 128), f32),
        ],
        scratch_shapes=[
            pltpu.VMEM(bt.shape, bf16),
            pltpu.VMEM((batches, HID, points), bf16),
            pltpu.VMEM((batches, SIGF, SIGF), bf16),
            pltpu.VMEM((HID, 2 * SEGS), f32),
            pltpu.VMEM((SEGS, 128), f32),
            pltpu.SemaphoreType.DMA((tiles,)),
            pltpu.SemaphoreType.DMA((tiles,)),
        ],
        compiler_params=pltpu.CompilerParams(vmem_limit_bytes=52 * MIB),
    )(scal, *rows, bt, w, atom, in_w, in_b, proj)


def second_kernel(
    scal_ref,
    x_ref,
    l1_ref,
    l2_ref,
    r1_ref,
    r2_ref,
    atom_in_ref,
    hw_ref,
    hb_ref,
    ow_ref,
    w_ref,
    atom_ref,
    hid_hbm,
    bt_hbm,
    out_ref,
    mats_ref,
    hid_ref,
    bt_ref,
    hw_t,
    feature,
    hid_sems,
    bt_sems,
):
    atom_start = scal_ref[9]
    tiles = tiles_of(bt_ref.shape[2], bt_ref.shape[0])
    hid_loads = fetch(hid_hbm, hid_ref, tiles, hid_sems)
    bt_loads = fetch(bt_hbm, bt_ref, tiles, bt_sems)
    for hid_load, bt_load in zip(hid_loads, bt_loads):
        hid_load.start()
        bt_load.start()

    def part(x, start, size):
        return x[:, start * CHIPA : (start + size) * CHIPA]

    zero = jnp.zeros((XROWS, 2 * CHIPA), f32)
    total = x_ref[:, :SEGS]
    total = total + jnp.concatenate([part(l1_ref, 1, 2), zero[:, :CHIPA]], axis=1)
    total = total + jnp.concatenate([part(l2_ref, 2, 1), zero], axis=1)
    total = total + jnp.concatenate([zero[:, :CHIPA], part(r1_ref, 0, 2)], axis=1)
    total = total + jnp.concatenate([zero, part(r2_ref, 0, 1)], axis=1)
    scaled = total[:ATW] / jnp.sqrt(total[ATW : ATW + 1] + eps_atom)
    value = jnp.dot(
        atom_in_ref[...].T, scaled.astype(bf16), preferred_element_type=f32
    )
    value = 0.5 * (value + hb_ref[...])
    high = value.astype(bf16)
    low = (value - high.astype(f32)).astype(bf16)
    feature[...] = jnp.concatenate([high, low], axis=1)
    hw_t[...] = (0.5 * hw_ref[...].astype(f32)).T.astype(bf16)
    mats_ref[...] = jnp.zeros_like(mats_ref)

    def weigh(i):
        b, cols = tiles[i]
        atom = atom_ref[b : b + 1, cols] - atom_start
        ids = lax.broadcasted_iota(jnp.int32, (SEGS, cols.size), 0)
        match = (ids == atom).astype(f32)
        member = jnp.concatenate([match, match], axis=0).astype(bf16)
        hid_loads[i].wait()
        half = jnp.dot(
            hw_t[...], hid_ref[b, :, cols], preferred_element_type=f32
        ) + jnp.dot(feature[...], member, preferred_element_type=f32)
        second = silu_of_twice(half)
        point = jnp.sum(second * ow_ref[...], axis=0, keepdims=True)
        scale = w_ref[b : b + 1, cols] * point
        bt_loads[i].wait()
        return (bt_ref[b, :, cols].astype(f32) * scale).astype(bf16)

    def gram(i, weighted):
        b, cols = tiles[i]
        mats_ref[b] += lax.dot_general(
            bt_ref[b, :, cols],
            weighted,
            (((1,), (1,)), ((), ())),
            preferred_element_type=f32,
        )

    for i in range(len(tiles)):
        gram(i, weigh(i))
    out_ref[...] = mats_ref[...].astype(bf16)


def second_pass(scal, sums, atom_in, hw, hb, ow, w, atom, hid, bt):
    batches, funcs, points = bt.shape
    tiles = len(tiles_of(points, batches))
    return pl.pallas_call(
        second_kernel,
        in_specs=[SMEM] + [VMEM] * 11 + [ANY] * 2,
        out_specs=VMEM,
        out_shape=jax.ShapeDtypeStruct((batches, SIGF, SIGF), bf16),
        scratch_shapes=[
            pltpu.VMEM((batches, SIGF, SIGF), f32),
            pltpu.VMEM(hid.shape, bf16),
            pltpu.VMEM(bt.shape, bf16),
            pltpu.VMEM((HID, HID), bf16),
            pltpu.VMEM((HID, 2 * SEGS), bf16),
            pltpu.SemaphoreType.DMA((tiles,)),
            pltpu.SemaphoreType.DMA((tiles,)),
        ],
        compiler_params=pltpu.CompilerParams(vmem_limit_bytes=52 * MIB),
    )(scal, *sums, atom_in, hw, hb, ow, w, atom, hid, bt)


def scatter(scal_ref, other_ref, mats_ref, got_ref, targets):
    core = scal_ref[8]
    for _, ref, _ in targets:
        ref[...] = jnp.zeros_like(ref)
    for blocks_ref, source in ((scal_ref, mats_ref), (other_ref, got_ref)):

        def place(i, _):
            b, k = i // SIGB, i % SIGB
            r = blocks_ref[i]
            here = (r % CHIPB) // 2 == core
            for chip, ref, first in targets:

                @pl.when((r // CHIPB == chip) & here)
                def _():
                    rows = block_of(r % 2)
                    for l in range(SIGB):
                        v = blocks_ref[b * SIGB + l]
                        cols = block_of(jnp.clip(v - first, 0, ref.shape[1] // FB - 1))
                        block = source[b, block_of(k), l * FB : (l + 1) * FB].astype(f32)
                        ref[rows, cols] = ref[rows, cols] + jnp.where(
                            near(r, v), block, jnp.zeros_like(block)
                        )

            return 0

        lax.fori_loop(0, source.shape[0] * SIGB, place, 0)


def side_kernel(
    scal_ref, other_ref, mats_ref, got_ref, left_ref, right_ref, to_left, to_right
):
    targets = ((0, to_left, 0), (2, to_right, CHIPB))
    scatter(scal_ref, other_ref, mats_ref, got_ref, targets)
    left_ref[...] = to_left[...].astype(bf16)
    right_ref[...] = to_right[...].astype(bf16)


def side_sums(scal, other, mats, got):
    side = jax.ShapeDtypeStruct((HALF, 2 * CHIPF), bf16)
    return pl.pallas_call(
        side_kernel,
        in_specs=[SMEM, SMEM, VMEM, VMEM],
        out_specs=[VMEM] * 2,
        out_shape=[side] * 2,
        scratch_shapes=[pltpu.VMEM((HALF, 2 * CHIPF), f32)] * 2,
        compiler_params=pltpu.CompilerParams(vmem_limit_bytes=20 * MIB),
    )(scal, other, mats, got)


def own_kernel(scal_ref, other_ref, mats_ref, got_ref, own_ref):
    scatter(scal_ref, other_ref, mats_ref, got_ref, ((1, own_ref, 0),))


def own_sums(scal, other, mats, got):
    return pl.pallas_call(
        own_kernel,
        in_specs=[SMEM, SMEM, VMEM, VMEM],
        out_specs=VMEM,
        out_shape=jax.ShapeDtypeStruct((HALF, 3 * CHIPF), f32),
        compiler_params=pltpu.CompilerParams(vmem_limit_bytes=20 * MIB),
        cost_estimate=pl.CostEstimate(
            flops=10**9, bytes_accessed=8 * mats.size, transcendentals=0
        ),
    )(scal, other, mats, got)


def final_kernel(own_ref, left_ref, right_ref, out_ref):
    chip = CHIPF
    out_ref[:, :chip] = own_ref[:, :chip] + left_ref[:, :chip].astype(f32)
    out_ref[:, chip : 2 * chip] = (
        own_ref[:, chip : 2 * chip]
        + left_ref[:, chip:].astype(f32)
        + right_ref[:, :chip].astype(f32)
    )
    out_ref[:, 2 * chip :] = own_ref[:, 2 * chip :] + right_ref[:, chip:].astype(f32)


def final_sum(own, left, right):
    rows, cols = own.shape
    strip = 128
    wide = pl.BlockSpec((strip, cols), lambda i: (i, 0))
    side = pl.BlockSpec((strip, 2 * CHIPF), lambda i: (i, 0))
    return pl.pallas_call(
        final_kernel,
        grid=(rows // strip,),
        in_specs=[wide, side, side],
        out_specs=wide,
        out_shape=jax.ShapeDtypeStruct((rows, cols), f32),
        compiler_params=pltpu.CompilerParams(vmem_limit_bytes=12 * MIB),
    )(own, left, right)


def on_device(
    basis_values,
    density,
    sig_blocks,
    grid_weights,
    atom_of,
    in_weight,
    in_bias,
    atom_proj,
    hidden_weight,
    atom_in,
    hidden_bias,
    out_weight,
):
    chips = lax.axis_size("pts")
    chip = lax.axis_index("pts")
    core = lax.axis_index("blk")

    def shift(x, by):
        return lax.ppermute(x, "pts", [(i, (i + by) % chips) for i in range(chips)])

    def swap(x):
        return lax.ppermute(x, "blk", [(0, 1), (1, 0)])

    scal = jnp.concatenate(
        [
            (sig_blocks - CHIPB * (chip - 1)).reshape(-1),
            core[None].astype(jnp.int32),
            (CHIPA * (chip - 1))[None].astype(jnp.int32),
        ]
    )
    from_left = shift(density[:, CHIPF:], 1)
    from_right = shift(density[:, : 2 * CHIPF], -1)
    sibling = swap(density)
    other = swap(scal)
    bt, token = transpose_basis(basis_values)
    side = jnp.concatenate([from_left, from_right], axis=0) + token
    side_sib = swap(side)

    column = lambda x, by=1.0: (by * x.astype(f32)).reshape(HID, 1)
    hidden, sums = first_pass(
        scal,
        (density, sibling, side, side_sib),
        bt,
        grid_weights,
        atom_of,
        column(in_weight, 0.5),
        column(in_bias, 0.5),
        atom_proj,
    )
    sums = sums + swap(sums)
    near_sums = {by: shift(sums, by) for by in (1, 2, -1, -2)}
    mats = second_pass(
        scal,
        [sums] + [near_sums[by] for by in (1, 2, -1, -2)],
        atom_in,
        hidden_weight,
        column(hidden_bias),
        column(out_weight),
        grid_weights,
        atom_of,
        hidden,
        bt,
    )
    got = swap(mats)
    to_left, to_right = side_sums(scal, other, mats, got)
    own = own_sums(scal, other, mats, got)
    return final_sum(own, shift(to_right, 1), shift(to_left, -1))


def solution(mesh):
    return jax.shard_map(
        on_device,
        mesh=mesh,
        in_specs=(
            P(("pts", "blk"), None, None),
            P(("pts", "blk"), None),
            P(("pts", "blk"), None),
            P(("pts", "blk"), None),
            P(("pts", "blk"), None),
            P(),
            P(),
            P(),
            P(),
            P(),
            P(),
            P(),
        ),
        out_specs=P(("pts", "blk"), None),
        check_vma=False,
    )
```

```python
import jax
import jax.numpy as jnp
from jax import lax
from jax.experimental import pallas as pl
from jax.experimental.pallas import tpu as pltpu
from jax.sharding import PartitionSpec as P

FB = 128
SIGB = 4
SIGF = 512
ATW = 64
HID = 256
CHIPB = 4
WINB = 12
HALF = 256
CHIPF = 512
CHIPA = 32
SEGS = 96
TILE = 2048
FIRST = (1024, 1024)
TRANS = 1024
MIB = 2**20
XROWS = 72

eps_atom = 0.0001
f32 = jnp.float32
bf16 = jnp.bfloat16

SMEM = pl.BlockSpec(memory_space=pltpu.SMEM)
VMEM = pl.BlockSpec(memory_space=pltpu.VMEM)
ANY = pl.BlockSpec(memory_space=pl.ANY)


def silu_of_twice(h):
    return h * (1.0 + jnp.tanh(h))


def block_of(i):
    return pl.ds(pl.multiple_of(i * FB, FB), FB)


def near(r, v):
    return jnp.abs(r // CHIPB - v // CHIPB) <= 1


def transpose_kernel(basis_ref, out_ref, token_ref):
    out_ref[0] = basis_ref[0].T
    token_ref[...] = jnp.zeros_like(token_ref)


def transpose_basis(basis):
    batches, points, funcs = basis.shape
    return pl.pallas_call(
        transpose_kernel,
        grid=(batches, points // TRANS),
        in_specs=[pl.BlockSpec((1, TRANS, funcs), lambda b, t: (b, t, 0))],
        out_specs=[
            pl.BlockSpec((1, funcs, TRANS), lambda b, t: (b, 0, t)),
            pl.BlockSpec((1, 2 * CHIPF), lambda b, t: (0, 0)),
        ],
        out_shape=[
            jax.ShapeDtypeStruct((batches, funcs, points), bf16),
            jax.ShapeDtypeStruct((1, 2 * CHIPF), bf16),
        ],
        compiler_params=pltpu.CompilerParams(vmem_limit_bytes=56 * MIB),
        cost_estimate=pl.CostEstimate(
            flops=10**10, bytes_accessed=4 * basis.size, transcendentals=0
        ),
    )(basis)


def tiles_of(points, batches):
    sizes = [[TILE] * (points // TILE) for _ in range(batches)]
    sizes[0] = list(FIRST) + sizes[0][1:]
    return [
        (b, pl.ds(sum(row[:i]), row[i])) for b, row in enumerate(sizes) for i in range(len(row))
    ]


def fetch(src, dst, tiles, sems):
    copies = [
        pltpu.make_async_copy(src.at[b, :, cols], dst.at[b, :, cols], sems.at[i])
        for i, (b, cols) in enumerate(tiles)
    ]
    return copies


def first_kernel(
    scal_ref,
    own_ref,
    sib_ref,
    side_ref,
    side_sib_ref,
    bt_hbm,
    w_ref,
    atom_ref,
    in_w_ref,
    in_b_ref,
    proj_ref,
    hid_hbm,
    sums_ref,
    bt_ref,
    hid_ref,
    sub,
    acc,
    squares,
    bt_sems,
    hid_sems,
):
    core = scal_ref[8]
    atom_start = scal_ref[9]
    batches = bt_ref.shape[0]
    tiles = tiles_of(bt_ref.shape[2], batches)
    loads = fetch(bt_hbm, bt_ref, tiles, bt_sems)
    stores = fetch(hid_ref, hid_hbm, tiles, hid_sems)
    for load in loads:
        load.start()
    sources = (
        (0, side_ref, side_sib_ref, 0, 0),
        (1, own_ref, sib_ref, 0, 0),
        (2, side_ref, side_sib_ref, 2, CHIPB),
    )

    def place(i, _):
        b, k = i // SIGB, i % SIGB
        r = scal_ref[i]
        here = (r % CHIPB) // 2 == core
        for chip, mine, other, row, first in sources:
            for ref, held in ((mine, here), (other, jnp.logical_not(here))):

                @pl.when((r // CHIPB == chip) & held)
                def _():
                    for l in range(SIGB):
                        v = scal_ref[b * SIGB + l]
                        col = jnp.clip(v - first, 0, ref.shape[1] // FB - 1)
                        block = ref[block_of(row + r % 2), block_of(col)]
                        sub[b, block_of(k), l * FB : (l + 1) * FB] = jnp.where(
                            near(r, v), block, jnp.zeros_like(block)
                        )

        return 0

    lax.fori_loop(0, batches * SIGB, place, 0)
    acc[...] = jnp.zeros_like(acc)
    squares[...] = jnp.zeros_like(squares)

    def density_at(i):
        b, cols = tiles[i]
        loads[i].wait()
        bt = bt_ref[b, :, cols]
        mixed = jnp.dot(sub[b], bt, preferred_element_type=f32)
        return jnp.sum(mixed * bt.astype(f32), axis=0, keepdims=True)

    def gather_sums(i, rho):
        b, cols = tiles[i]
        hidden = silu_of_twice(rho * in_w_ref[...] + in_b_ref[...]).astype(bf16)
        hid_ref[b, :, cols] = hidden
        stores[i].start()
        w = w_ref[b : b + 1, cols]
        atom = atom_ref[b : b + 1, cols] - atom_start
        w_high = w.astype(bf16).astype(f32)
        w_low = w - w_high
        match = lax.broadcasted_iota(jnp.int32, (SEGS, cols.size), 0) == atom
        zero = jnp.zeros((SEGS, cols.size), f32)
        member = jnp.concatenate(
            [jnp.where(match, w_high, zero), jnp.where(match, w_low, zero)], axis=0
        ).astype(bf16)
        acc[...] += lax.dot_general(
            hidden, member, (((1,), (1,)), ((), ())), preferred_element_type=f32
        )
        part = jnp.where(match, w * w, zero)
        total = part[:, :128]
        for j in range(1, cols.size // 128):
            total = total + part[:, j * 128 : (j + 1) * 128]
        squares[...] += total

    for i in range(len(tiles)):
        gather_sums(i, density_at(i))
    weighted = acc[:, :SEGS] + acc[:, SEGS:]
    sums = jnp.dot(
        proj_ref[...].astype(f32).T,
        weighted,
        precision=lax.Precision.HIGHEST,
        preferred_element_type=f32,
    )
    sums_ref[...] = jnp.zeros_like(sums_ref)
    sums_ref[:ATW, :SEGS] = sums
    row = jnp.sum(squares[...].T, axis=0, keepdims=True)
    sums_ref[ATW : ATW + 1, :SEGS] = row
    for store in stores:
        store.wait()


def first_pass(scal, rows, bt, w, atom, in_w, in_b, proj):
    batches, funcs, points = bt.shape
    tiles = len(tiles_of(points, batches))
    return pl.pallas_call(
        first_kernel,
        in_specs=[SMEM] + [VMEM] * 4 + [ANY] + [VMEM] * 5,
        out_specs=[ANY, VMEM],
        out_shape=[
            jax.ShapeDtypeStruct((batches, HID, points), bf16),
            jax.ShapeDtypeStruct((XROWS, 128), f32),
        ],
        scratch_shapes=[
            pltpu.VMEM(bt.shape, bf16),
            pltpu.VMEM((batches, HID, points), bf16),
            pltpu.VMEM((batches, SIGF, SIGF), bf16),
            pltpu.VMEM((HID, 2 * SEGS), f32),
            pltpu.VMEM((SEGS, 128), f32),
            pltpu.SemaphoreType.DMA((tiles,)),
            pltpu.SemaphoreType.DMA((tiles,)),
        ],
        compiler_params=pltpu.CompilerParams(vmem_limit_bytes=52 * MIB),
    )(scal, *rows, bt, w, atom, in_w, in_b, proj)


def second_kernel(
    scal_ref,
    x_ref,
    l1_ref,
    l2_ref,
    r1_ref,
    r2_ref,
    atom_in_ref,
    hw_ref,
    hb_ref,
    ow_ref,
    w_ref,
    atom_ref,
    hid_hbm,
    bt_hbm,
    out_ref,
    mats_ref,
    hid_ref,
    bt_ref,
    hw_t,
    feature,
    hid_sems,
    bt_sems,
):
    atom_start = scal_ref[9]
    tiles = tiles_of(bt_ref.shape[2], bt_ref.shape[0])
    hid_loads = fetch(hid_hbm, hid_ref, tiles, hid_sems)
    bt_loads = fetch(bt_hbm, bt_ref, tiles, bt_sems)
    for hid_load, bt_load in zip(hid_loads, bt_loads):
        hid_load.start()
        bt_load.start()

    def part(x, start, size):
        return x[:, start * CHIPA : (start + size) * CHIPA]

    zero = jnp.zeros((XROWS, 2 * CHIPA), f32)
    total = x_ref[:, :SEGS]
    total = total + jnp.concatenate([part(l1_ref, 1, 2), zero[:, :CHIPA]], axis=1)
    total = total + jnp.concatenate([part(l2_ref, 2, 1), zero], axis=1)
    total = total + jnp.concatenate([zero[:, :CHIPA], part(r1_ref, 0, 2)], axis=1)
    total = total + jnp.concatenate([zero, part(r2_ref, 0, 1)], axis=1)
    scaled = total[:ATW] / jnp.sqrt(total[ATW : ATW + 1] + eps_atom)
    value = jnp.dot(
        atom_in_ref[...].T, scaled.astype(bf16), preferred_element_type=f32
    )
    value = 0.5 * (value + hb_ref[...])
    high = value.astype(bf16)
    low = (value - high.astype(f32)).astype(bf16)
    feature[...] = jnp.concatenate([high, low], axis=1)
    hw_t[...] = (0.5 * hw_ref[...].astype(f32)).T.astype(bf16)
    mats_ref[...] = jnp.zeros_like(mats_ref)

    def weigh(i):
        b, cols = tiles[i]
        atom = atom_ref[b : b + 1, cols] - atom_start
        ids = lax.broadcasted_iota(jnp.int32, (SEGS, cols.size), 0)
        match = (ids == atom).astype(f32)
        member = jnp.concatenate([match, match], axis=0).astype(bf16)
        hid_loads[i].wait()
        half = jnp.dot(
            hw_t[...], hid_ref[b, :, cols], preferred_element_type=f32
        ) + jnp.dot(feature[...], member, preferred_element_type=f32)
        second = silu_of_twice(half)
        point = jnp.sum(second * ow_ref[...], axis=0, keepdims=True)
        scale = w_ref[b : b + 1, cols] * point
        bt_loads[i].wait()
        return (bt_ref[b, :, cols].astype(f32) * scale).astype(bf16)

    def gram(i, weighted):
        b, cols = tiles[i]
        mats_ref[b] += lax.dot_general(
            bt_ref[b, :, cols],
            weighted,
            (((1,), (1,)), ((), ())),
            preferred_element_type=f32,
        )

    for i in range(len(tiles)):
        gram(i, weigh(i))
    out_ref[...] = mats_ref[...].astype(bf16)


def second_pass(scal, sums, atom_in, hw, hb, ow, w, atom, hid, bt):
    batches, funcs, points = bt.shape
    tiles = len(tiles_of(points, batches))
    return pl.pallas_call(
        second_kernel,
        in_specs=[SMEM] + [VMEM] * 11 + [ANY] * 2,
        out_specs=VMEM,
        out_shape=jax.ShapeDtypeStruct((batches, SIGF, SIGF), bf16),
        scratch_shapes=[
            pltpu.VMEM((batches, SIGF, SIGF), f32),
            pltpu.VMEM(hid.shape, bf16),
            pltpu.VMEM(bt.shape, bf16),
            pltpu.VMEM((HID, HID), bf16),
            pltpu.VMEM((HID, 2 * SEGS), bf16),
            pltpu.SemaphoreType.DMA((tiles,)),
            pltpu.SemaphoreType.DMA((tiles,)),
        ],
        compiler_params=pltpu.CompilerParams(vmem_limit_bytes=52 * MIB),
    )(scal, *sums, atom_in, hw, hb, ow, w, atom, hid, bt)


def scatter(scal_ref, other_ref, mats_ref, got_ref, targets):
    core = scal_ref[8]
    for _, ref, _ in targets:
        ref[...] = jnp.zeros_like(ref)
    for blocks_ref, source in ((scal_ref, mats_ref), (other_ref, got_ref)):

        def place(i, _):
            b, k = i // SIGB, i % SIGB
            r = blocks_ref[i]
            here = (r % CHIPB) // 2 == core
            for chip, ref, first in targets:

                @pl.when((r // CHIPB == chip) & here)
                def _():
                    rows = block_of(r % 2)
                    for l in range(SIGB):
                        v = blocks_ref[b * SIGB + l]
                        cols = block_of(jnp.clip(v - first, 0, ref.shape[1] // FB - 1))
                        block = source[b, block_of(k), l * FB : (l + 1) * FB].astype(f32)
                        ref[rows, cols] = ref[rows, cols] + jnp.where(
                            near(r, v), block, jnp.zeros_like(block)
                        )

            return 0

        lax.fori_loop(0, source.shape[0] * SIGB, place, 0)


def side_kernel(
    scal_ref, other_ref, mats_ref, got_ref, left_ref, right_ref, to_left, to_right
):
    targets = ((0, to_left, 0), (2, to_right, CHIPB))
    scatter(scal_ref, other_ref, mats_ref, got_ref, targets)
    left_ref[...] = to_left[...].astype(bf16)
    right_ref[...] = to_right[...].astype(bf16)


def side_sums(scal, other, mats, got):
    side = jax.ShapeDtypeStruct((HALF, 2 * CHIPF), bf16)
    return pl.pallas_call(
        side_kernel,
        in_specs=[SMEM, SMEM, VMEM, VMEM],
        out_specs=[VMEM] * 2,
        out_shape=[side] * 2,
        scratch_shapes=[pltpu.VMEM((HALF, 2 * CHIPF), f32)] * 2,
        compiler_params=pltpu.CompilerParams(vmem_limit_bytes=20 * MIB),
    )(scal, other, mats, got)


def own_kernel(scal_ref, other_ref, mats_ref, got_ref, own_ref):
    scatter(scal_ref, other_ref, mats_ref, got_ref, ((1, own_ref, 0),))


def own_sums(scal, other, mats, got):
    return pl.pallas_call(
        own_kernel,
        in_specs=[SMEM, SMEM, VMEM, VMEM],
        out_specs=VMEM,
        out_shape=jax.ShapeDtypeStruct((HALF, 3 * CHIPF), f32),
        compiler_params=pltpu.CompilerParams(vmem_limit_bytes=20 * MIB),
        cost_estimate=pl.CostEstimate(
            flops=10**9, bytes_accessed=8 * mats.size, transcendentals=0
        ),
    )(scal, other, mats, got)


def final_kernel(own_ref, left_ref, right_ref, out_ref):
    chip = CHIPF
    out_ref[:, :chip] = own_ref[:, :chip] + left_ref[:, :chip].astype(f32)
    out_ref[:, chip : 2 * chip] = (
        own_ref[:, chip : 2 * chip]
        + left_ref[:, chip:].astype(f32)
        + right_ref[:, :chip].astype(f32)
    )
    out_ref[:, 2 * chip :] = own_ref[:, 2 * chip :] + right_ref[:, chip:].astype(f32)


def final_sum(own, left, right):
    rows, cols = own.shape
    strip = 128
    wide = pl.BlockSpec((strip, cols), lambda i: (i, 0))
    side = pl.BlockSpec((strip, 2 * CHIPF), lambda i: (i, 0))
    return pl.pallas_call(
        final_kernel,
        grid=(rows // strip,),
        in_specs=[wide, side, side],
        out_specs=wide,
        out_shape=jax.ShapeDtypeStruct((rows, cols), f32),
        compiler_params=pltpu.CompilerParams(vmem_limit_bytes=12 * MIB),
    )(own, left, right)


def on_device(
    basis_values,
    density,
    sig_blocks,
    grid_weights,
    atom_of,
    in_weight,
    in_bias,
    atom_proj,
    hidden_weight,
    atom_in,
    hidden_bias,
    out_weight,
):
    chips = lax.axis_size("pts")
    chip = lax.axis_index("pts")
    core = lax.axis_index("blk")

    def shift(x, by):
        return lax.ppermute(x, "pts", [(i, (i + by) % chips) for i in range(chips)])

    def swap(x):
        return lax.ppermute(x, "blk", [(0, 1), (1, 0)])

    scal = jnp.concatenate(
        [
            (sig_blocks - CHIPB * (chip - 1)).reshape(-1),
            core[None].astype(jnp.int32),
            (CHIPA * (chip - 1))[None].astype(jnp.int32),
        ]
    )
    from_left = shift(density[:, CHIPF:], 1)
    from_right = shift(density[:, : 2 * CHIPF], -1)
    sibling = swap(density)
    other = swap(scal)
    bt, token = transpose_basis(basis_values)
    side = jnp.concatenate([from_left, from_right], axis=0) + (token + 0 * sibling[:1, : 2 * CHIPF])
    side_sib = swap(side)

    column = lambda x, by=1.0: (by * x.astype(f32)).reshape(HID, 1)
    hidden, sums = first_pass(
        scal,
        (density, sibling, side, side_sib),
        bt,
        grid_weights,
        atom_of,
        column(in_weight, 0.5),
        column(in_bias, 0.5),
        atom_proj,
    )
    sums = sums + swap(sums)
    near_sums = {by: shift(sums, by) for by in (1, 2, -1, -2)}
    mats = second_pass(
        scal,
        [sums] + [near_sums[by] for by in (1, 2, -1, -2)],
        atom_in,
        hidden_weight,
        column(hidden_bias),
        column(out_weight),
        grid_weights,
        atom_of,
        hidden,
        bt,
    )
    got = swap(mats)
    to_left, to_right = side_sums(scal, other, mats, got)
    own = own_sums(scal, other, mats, got)
    return final_sum(own, shift(to_right, 1), shift(to_left, -1))


def solution(mesh):
    return jax.shard_map(
        on_device,
        mesh=mesh,
        in_specs=(
            P(("pts", "blk"), None, None),
            P(("pts", "blk"), None),
            P(("pts", "blk"), None),
            P(("pts", "blk"), None),
            P(("pts", "blk"), None),
            P(),
            P(),
            P(),
            P(),
            P(),
            P(),
            P(),
        ),
        out_specs=P(("pts", "blk"), None),
        check_vma=False,
    )
```
